32 devices in a mesh: wall: 4 (over y, x), gas: 8 (over z, core).
Axes of the slice: x: 2, y: 2, z: 4, core: 2. Of those that a mesh axis runs over, the one named last changes fastest.
Arguments:
- gas_state: float32 [3, 4, 512, 4096], P(None, None, 'wall', 'gas'), may hold values from -8 to 8
- wall_flags: int32 [512, 32], P('wall', 'gas'), may hold values from 0 to 128
- film_state: float32 [4, 512, 4096], P(None, 'wall', 'gas'), may hold values from -12 to 12, as said below
- deposit: float32 [512, 4096], P('wall', 'gas'), may hold values from 0.05 to 1
- owner_map: int32 [4, 8], replicated, may hold values from 0 to 7, each once within a row
Outputs:
- film_out: float32 [4, 512, 4096], P(None, ('wall', 'gas'))
- cfl: float32 [], replicated
The draws below stay inside these ranges and needn't reach their ends.
Inputs may be any that keep to these rules, and one draw needn't show every extreme that they name: film_state[0] is positive. `owner_map`: each row is a permutation of 0 to 8 - 1.
All inputs are finite; a program needn't handle non-finite values.
Results may differ from the reference program's by a relative error of at most 0.00002.
Values sent between devices are 32-bit elements; how exact they have to be, the bound alone decides.
A program may use at most 64 MiB of HBM per device.

```python
import math
import jax
import jax.numpy as jnp

LAYERS = 4
SUBSTEPS = 4
WY = 512
WX = 4096
STRIP = 16
N_WALL = 4
N_GAS = 8


def draw_film_state(key, part):
    subkeys = jax.random.split(key, 5)
    row_share = jnp.arange(WY, dtype=jnp.float32) / max(WY - 1, 1)
    col_share = jnp.arange(WX, dtype=jnp.float32) / max(WX - 1, 1)
    rising = jnp.exp(jnp.log(3.0) * 0.5 * (row_share[:, None] + col_share[None, :]))
    roughness = jax.random.uniform(subkeys[4], (WY, WX), jnp.float32, 0.5, 1.0)
    height = jax.random.uniform(subkeys[0], (WY, WX), jnp.float32, 0.2, 1.5)
    momentum = jnp.clip(jax.random.normal(subkeys[1], (2, WY, WX), jnp.float32), -4.0, 4.0)
    film_heat = jnp.clip(jax.random.normal(subkeys[2], (WY, WX), jnp.float32), -4.0, 4.0)
    momentum = momentum * (rising * roughness)[None]
    return jnp.stack([height, momentum[0], momentum[1], film_heat]).astype(jnp.float32)


def place_ends(result, own_key, least, high):
    place = [jax.random.randint(jax.random.fold_in(own_key, axis), (), 0, length) for axis, length in enumerate(result.shape)]
    main_axis = result.shape.index(max(result.shape))
    next_to = place[:main_axis] + [(place[main_axis] + 1) % result.shape[main_axis]] + place[main_axis + 1:]
    return result.at[tuple(place)].set(least).at[tuple(next_to)].set(high)


def level_of(own_key, extent, cuts, smallest, largest):
    factor_of = 1.0
    for dim, shards_of in cuts:
        heights = jax.random.uniform(jax.random.fold_in(jax.random.fold_in(own_key, 6), dim), (shards_of,), jnp.float32, smallest / len(cuts), largest / len(cuts))
        factor_of = factor_of * jnp.repeat(jnp.exp(heights), extent[dim] // shards_of).reshape((-1,) + (1,) * (len(extent) - 1 - dim))
    return factor_of


def gaussian(stream_key, extent, scale, most, cuts=(), kind=jnp.bfloat16):
    loudness = level_of(stream_key, extent, cuts, -0.22, 0.18) if cuts else 1.0
    drawn = jax.random.normal(stream_key, extent, jnp.float32) * scale * loudness
    return jnp.minimum(jnp.maximum(drawn, -most), most).astype(kind)


def setup_inputs(seed: int = 0) -> dict:
    keys = jax.random.split(jax.random.key(seed), 6)
    gas_state = gaussian(keys[0], (3, LAYERS, WY, WX), 1.5, 8.0, ((2, 4), (3, 8)), jnp.float32)
    wall_flags = place_ends(jax.random.randint(keys[1], (WY, WX // 128), 0, 129), jax.random.fold_in(keys[1], 1), 0, 128).astype(jnp.int32)
    film_state = draw_film_state(jax.random.fold_in(keys[5], 71), 0)
    deposit = jnp.clip(jnp.exp(math.log(1.0) - 2.9957323 * jax.random.uniform(keys[3], (WY, WX), jnp.float32) ** level_of(keys[3], (WY, WX), ((0, 4), (1, 8)), -0.2, 0.2)), 0.05, 1.0)
    owner_map = jax.vmap(lambda own: jax.random.permutation(own, N_GAS))(jax.random.split(keys[4], N_WALL)).reshape((N_WALL, N_GAS)).astype(jnp.int32)
    return {"gas_state": gas_state, "wall_flags": wall_flags, "film_state": film_state, "deposit": deposit, "owner_map": owner_map}


LAYER_WEIGHTS = (0.1, 0.2, 0.3, 0.4)
KAPPA = 0.41
HEIGHT_RATIO = 20.0
SPEED_FLOOR = 0.5
PRANDTL_TURB = 0.85
PRANDTL_JUMP = 3.0
LAMINAR_SHEAR = 0.3
LAMINAR_HEAT = 0.2
FILM_SPREAD = 0.24
FILM_FLOOR = 0.3
FRICTION = 0.5
GRAVITY = 1.0
COURANT = 6.0

def reichardt(scaled_height):
    return jnp.log1p(KAPPA * scaled_height) / KAPPA + 7.8 * (1.0 - jnp.exp(-scaled_height / 11.0) - scaled_height / 11.0 * jnp.exp(-scaled_height / 3.0))

def surface_forcing(filtered, film_heat, attached, deposit):
    along, across, gas_heat = (filtered[0], filtered[1], filtered[2])
    wall_speed = jnp.sqrt(along * along + across * across + SPEED_FLOOR * SPEED_FLOOR)
    scaled_height = jnp.sqrt(HEIGHT_RATIO * wall_speed)
    scaled_speed = reichardt(scaled_height)
    factor = wall_speed / (scaled_speed * scaled_speed)
    contrast = gas_heat - film_heat
    shear_along = jnp.where(attached, factor * along, LAMINAR_SHEAR * along)
    shear_across = jnp.where(attached, factor * across, LAMINAR_SHEAR * across)
    heat_flux = jnp.where(attached, wall_speed * contrast / (PRANDTL_TURB * scaled_speed + PRANDTL_JUMP), LAMINAR_HEAT * contrast)
    return jnp.stack([shear_along, shear_across, heat_flux, deposit])

def peak_speed(film_now):
    thickness = jnp.sqrt(film_now[0] * film_now[0] + FILM_FLOOR * FILM_FLOOR)
    moving = jnp.sqrt(film_now[1] * film_now[1] + film_now[2] * film_now[2])
    return jnp.max(moving / thickness + jnp.sqrt(GRAVITY * thickness))

def advance(padded, forcing, time_step):
    centre = padded[:, 1:-1, 1:-1]
    north_side = padded[:, :-2, 1:-1]
    south_side = padded[:, 2:, 1:-1]
    west_side = padded[:, 1:-1, :-2]
    east_side = padded[:, 1:-1, 2:]
    spread = north_side + south_side + west_side + east_side - 4.0 * centre
    height = centre[0]
    thickness = jnp.sqrt(height * height + FILM_FLOOR * FILM_FLOOR)
    divergence = 0.5 * (east_side[1] - west_side[1]) + 0.5 * (south_side[2] - north_side[2])
    slope_along = 0.5 * (east_side[0] - west_side[0])
    slope_across = 0.5 * (south_side[0] - north_side[0])
    new_height = height + FILM_SPREAD * spread[0] + time_step * (forcing[3] - divergence)
    new_along = centre[1] + FILM_SPREAD * spread[1] + time_step * (forcing[0] - FRICTION * centre[1] / thickness - GRAVITY * height * slope_along)
    new_across = centre[2] + FILM_SPREAD * spread[2] + time_step * (forcing[1] - FRICTION * centre[2] / thickness - GRAVITY * height * slope_across)
    new_heat = centre[3] + FILM_SPREAD * spread[3] + time_step * forcing[2] / thickness
    return jnp.stack([new_height, new_along, new_across, new_heat])

def reference(gas_state, wall_flags, film_state, deposit, owner_map):
    sampled = LAYER_WEIGHTS[0] * gas_state[:, 0]
    for layer in range(1, LAYERS):
        sampled = sampled + LAYER_WEIGHTS[layer] * gas_state[:, layer]
    row_sum = jnp.roll(sampled, 1, 1) + sampled + jnp.roll(sampled, -1, 1)
    filtered = (jnp.roll(row_sum, 1, 2) + row_sum + jnp.roll(row_sum, -1, 2)) / 9.0
    limit = jnp.repeat(wall_flags, 128, axis=1)
    position = jnp.arange(WX, dtype=jnp.int32) % 128
    attached = position[None, :] < limit
    forcing = surface_forcing(filtered, film_state[3], attached, deposit)
    time_step = COURANT / peak_speed(film_state)
    film_now = film_state
    for substep in range(SUBSTEPS):
        film_now = advance(jnp.pad(film_now, ((0, 0), (1, 1), (1, 1)), mode='wrap'), forcing, time_step)
    cfl = time_step * peak_speed(film_now)
    inverse = jnp.argsort(owner_map, axis=1).astype(jnp.int32)
    strips = film_now.reshape(4, N_WALL, N_GAS, STRIP, WX)
    bands = jnp.arange(N_WALL, dtype=jnp.int32)
    picked = strips[:, bands[:, None], inverse]
    return (picked.reshape(4, WY, WX), cfl)
```

```python
import functools

import jax
import jax.numpy as jnp
from jax import lax
from jax.experimental import pallas as pl
from jax.experimental.pallas import tpu as pltpu
from jax.sharding import PartitionSpec as P

SUBSTEPS = 4
HALO = SUBSTEPS
LANES = 128
SUBLANES = 8

LAYER_WEIGHTS = (0.1, 0.2, 0.3, 0.4)
KAPPA = 0.41
HEIGHT_RATIO = 20.0
SPEED_FLOOR = 0.5
PRANDTL_TURB = 0.85
PRANDTL_JUMP = 3.0
LAMINAR_SHEAR = 0.3
LAMINAR_HEAT = 0.2
FILM_SPREAD = 0.24
FILM_FLOOR = 0.3
FRICTION = 0.5
GRAVITY = 1.0
COURANT = 6.0

FILM, GAS, DEPOSIT, ATTACHED, FIELDS = 0, 4, 7, 8, 9
MESH = pl.DeviceIdType.MESH


def reichardt(scaled_height):
    return jnp.log(1.0 + KAPPA * scaled_height) * (1.0 / KAPPA) + 7.8 * (
        1.0
        - jnp.exp(scaled_height * (-1.0 / 11.0))
        - scaled_height * (1.0 / 11.0) * jnp.exp(scaled_height * (-1.0 / 3.0))
    )


def speed_measure(height, along, across):
    squared = height * height + FILM_FLOOR * FILM_FLOOR
    inverse = lax.rsqrt(squared)
    thickness = squared * inverse
    return jnp.sqrt(along * along + across * across) * inverse + jnp.sqrt(GRAVITY * thickness)


def tile_max(value):
    tiles = [
        value[r : r + SUBLANES, c : c + LANES]
        for r in range(0, value.shape[0], SUBLANES)
        for c in range(0, value.shape[1], LANES)
    ]
    while len(tiles) > 1:
        tiles = [jnp.maximum(a, b) for a, b in zip(tiles[::2], tiles[1::2])] + (
            [tiles[-1]] if len(tiles) % 2 else []
        )
    return tiles[0]


def kernel(
    n_wall, n_gas,
    gas_hbm, flags_hbm, film_hbm, deposit_hbm, owner_hbm,
    out_ref, cfl_ref,
    gas, flags, film, deposit, owner, ext, held, outbox,
    from_north, from_south, east_side, west_side, pack_east, pack_west, corner,
    peak_send, peak_gas, peak_wall,
    load_sem, halo_send, halo_recv, peak_gas_send, peak_gas_recv, peak_wall_send, peak_wall_recv,
    strip_send, strip_recv, own_sem,
):
    rows, cols = film.shape[1], film.shape[2]
    wide = cols + LANES
    strip = rows // n_gas
    block = strip + 2 * HALO
    w, g = lax.axis_index("wall"), lax.axis_index("gas")
    north, south = (w + n_wall - 1) % n_wall, (w + 1) % n_wall
    west, east = (g + n_gas - 1) % n_gas, (g + 1) % n_gas

    loads = [
        pltpu.make_async_copy(film_hbm, film, load_sem.at[0]),
        pltpu.make_async_copy(flags_hbm, flags, load_sem.at[1]),
        pltpu.make_async_copy(deposit_hbm, deposit, load_sem.at[2]),
        pltpu.make_async_copy(owner_hbm, owner, load_sem.at[3]),
    ] + [
        pltpu.make_async_copy(gas_hbm.at[c], gas.at[c], load_sem.at[4 + c]) for c in range(3)
    ]
    for load in loads:
        load.start()

    barrier = pltpu.get_barrier_semaphore()
    peers = (
        [(w, (g + k) % n_gas) for k in range(1, n_gas)]
        + [((w + k) % n_wall, g) for k in range(1, n_wall)]
        + [(a, b) for a in (north, south) for b in (west, east)]
    )
    for peer in peers:
        pl.semaphore_signal(barrier, inc=1, device_id=peer, device_id_type=MESH)

    def gas_peaks(turn):
        return [
            pltpu.make_async_remote_copy(
                src_ref=peak_send.at[turn, 0],
                dst_ref=peak_gas.at[turn, k - 1],
                send_sem=peak_gas_send.at[turn, k - 1],
                recv_sem=peak_gas_recv.at[turn, k - 1],
                device_id=(w, (g + k) % n_gas),
                device_id_type=MESH,
            )
            for k in range(1, n_gas)
        ]

    def wall_peaks(turn):
        return [
            pltpu.make_async_remote_copy(
                src_ref=peak_send.at[turn, 1],
                dst_ref=peak_wall.at[turn, k - 1],
                send_sem=peak_wall_send.at[turn, k - 1],
                recv_sem=peak_wall_recv.at[turn, k - 1],
                device_id=((w + k) % n_wall, g),
                device_id_type=MESH,
            )
            for k in range(1, n_wall)
        ]

    def middle(turn, own_peak, copies):
        for copy in copies:
            copy.wait_recv()
        for k in range(n_gas - 1):
            own_peak = jnp.maximum(own_peak, peak_gas[turn, k])
        peak_send[turn, 1] = own_peak
        later = wall_peaks(turn)
        for copy in later:
            copy.start()
        return later

    def finish(turn, copies):
        for copy in copies:
            copy.wait_recv()
        whole = peak_send[turn, 1]
        for k in range(n_wall - 1):
            whole = jnp.maximum(whole, peak_wall[turn, k])
        return jnp.max(whole)

    loads[0].wait()
    peak_send[0, 0] = tile_max(speed_measure(film[0], film[1], film[2]))
    pl.semaphore_wait(barrier, len(peers))
    first_gas = gas_peaks(0)
    for copy in first_gas:
        copy.start()

    own_rows = slice(HALO, HALO + rows)
    for f in range(4):
        ext[FILM + f, own_rows, 0:cols] = film[f]
    loads[1].wait()
    lane_own = lax.broadcasted_iota(jnp.int32, (rows, LANES), 1)
    for s in range(cols // LANES):
        ext[ATTACHED, own_rows, s * LANES : (s + 1) * LANES] = jnp.where(
            lane_own < flags[:, s : s + 1], 1.0, 0.0
        )
    loads[2].wait()
    ext[DEPOSIT, own_rows, 0:cols] = deposit[...]
    for c in range(3):
        loads[4 + c].wait()
        sampled = LAYER_WEIGHTS[0] * gas[c, 0]
        for layer in range(1, gas.shape[1]):
            sampled = sampled + LAYER_WEIGHTS[layer] * gas[c, layer]
        ext[GAS + c, own_rows, 0:cols] = sampled

    tall = rows + 2 * HALO
    lane = lax.broadcasted_iota(jnp.int32, (tall, LANES), 1)
    to_west = ext[0, :, 0:LANES]
    to_east = pltpu.roll(ext[0, :, cols - LANES : cols], HALO, 1)
    for f in range(1, FIELDS):
        here = lane >= HALO * f
        to_west = jnp.where(here, pltpu.roll(ext[f, :, 0:LANES], HALO * f, 1), to_west)
        to_east = jnp.where(
            here, pltpu.roll(ext[f, :, cols - LANES : cols], HALO * (f + 1), 1), to_east
        )
    pack_west[...] = to_west
    pack_east[...] = to_east

    top, bottom = pl.ds(0, SUBLANES), pl.ds(tall - SUBLANES, SUBLANES)

    def halo(index, src, dst, device):
        return pltpu.make_async_remote_copy(
            src_ref=src, dst_ref=dst, send_sem=halo_send.at[index], recv_sem=halo_recv.at[index],
            device_id=device, device_id_type=MESH,
        )

    halos = [
        halo(0, ext.at[:, top, pl.ds(0, cols)], from_south, (north, g)),
        halo(1, ext.at[:, bottom, pl.ds(0, cols)], from_north, (south, g)),
        halo(2, pack_west, east_side, (w, west)),
        halo(3, pack_east, west_side, (w, east)),
        halo(4, pack_west.at[top], corner.at[0], (north, west)),
        halo(5, pack_west.at[bottom], corner.at[1], (south, west)),
        halo(6, pack_east.at[top], corner.at[2], (north, east)),
        halo(7, pack_east.at[bottom], corner.at[3], (south, east)),
    ]
    for copy in halos:
        copy.start()

    first_wall = middle(0, peak_send[0, 0], first_gas)

    for copy in halos:
        copy.wait()
    for f in range(FIELDS):
        ext[f, 0:HALO, 0:cols] = from_north[f, 0:HALO]
        ext[f, tall - HALO : tall, 0:cols] = from_south[f, HALO : 2 * HALO]
    east_side[tall - HALO : tall] = corner[0, HALO : 2 * HALO]
    east_side[0:HALO] = corner[1, 0:HALO]
    west_side[tall - HALO : tall] = corner[2, HALO : 2 * HALO]
    west_side[0:HALO] = corner[3, 0:HALO]
    for f in range(FIELDS):
        ext[f, :, cols:wide] = jnp.where(
            lane < HALO,
            pltpu.roll(east_side[...], (LANES - HALO * f) % LANES, 1),
            pltpu.roll(west_side[...], LANES - HALO - HALO * f, 1),
        )

    tiles = tall // SUBLANES
    sub = lax.broadcasted_iota(jnp.int32, (SUBLANES, wide), 0)

    def force_tile(i, carry):
        now = pl.ds(pl.multiple_of(i * SUBLANES, SUBLANES), SUBLANES)
        above = pl.ds(pl.multiple_of((i + tiles - 1) % tiles * SUBLANES, SUBLANES), SUBLANES)
        below = pl.ds(pl.multiple_of((i + 1) % tiles * SUBLANES, SUBLANES), SUBLANES)

        def filtered(f):
            centre = ext[f, now, :]
            up = jnp.where(sub == 0, pltpu.roll(ext[f, above, :], 1, 0), pltpu.roll(centre, 1, 0))
            down = jnp.where(
                sub == SUBLANES - 1,
                pltpu.roll(ext[f, below, :], SUBLANES - 1, 0),
                pltpu.roll(centre, SUBLANES - 1, 0),
            )
            total = up + centre + down
            return (pltpu.roll(total, 1, 1) + total + pltpu.roll(total, wide - 1, 1)) * (1.0 / 9.0)

        along, across, gas_heat = filtered(GAS), filtered(GAS + 1), filtered(GAS + 2)
        attached = ext[ATTACHED, now, :] > 0.5
        wall_speed = jnp.sqrt(along * along + across * across + SPEED_FLOOR * SPEED_FLOOR)
        scaled_speed = reichardt(jnp.sqrt(HEIGHT_RATIO * wall_speed))
        contrast = gas_heat - ext[FILM + 3, now, :]
        factor = jnp.where(attached, wall_speed / (scaled_speed * scaled_speed), LAMINAR_SHEAR)
        for f in range(4):
            held[f, i] = ext[FILM + f, now, :]
        held[4, i] = factor * along
        held[5, i] = factor * across
        held[7, i] = ext[DEPOSIT, now, :]
        held[6, i] = contrast * jnp.where(
            attached, wall_speed / (PRANDTL_TURB * scaled_speed + PRANDTL_JUMP), LAMINAR_HEAT
        )
        return carry

    lax.fori_loop(0, tiles, force_tile, 0)

    time_step = COURANT / finish(0, first_wall)
    half = 0.5 * time_step
    loads[3].wait()

    def offset(i):
        return n_gas // 2 + (i + 1) // 2 * (1 - 2 * (i % 2))

    def strip_copy(i):
        return pltpu.make_async_remote_copy(
            src_ref=outbox.at[i],
            dst_ref=out_ref.at[:, :, pl.ds(pl.multiple_of(g * cols, LANES), cols)],
            send_sem=strip_send.at[i],
            recv_sem=strip_recv.at[i],
            device_id=(w, (g + offset(i)) % n_gas),
            device_id_type=MESH,
        )

    def advance_strip(i, peak):
        target = (g + offset(i)) % n_gas
        which = jnp.int32(0)
        for j in range(n_gas):
            match = 1 - jnp.minimum(jnp.abs(owner[w, j] - target), 1)
            which = jnp.maximum(which, j * match)
        first = which * (strip // SUBLANES)

        def window(f):
            return jnp.concatenate([held[f, first + t] for t in range(block // SUBLANES)], axis=0)

        push_along = time_step * window(4)
        push_across = time_step * window(5)
        heating = time_step * window(6)
        spray = time_step * window(7)

        def sides(value):
            return (
                pltpu.roll(value, 1, 0),
                pltpu.roll(value, block - 1, 0),
                pltpu.roll(value, 1, 1),
                pltpu.roll(value, wide - 1, 1),
            )

        def spread(value, n, s, ww, e):
            return (1.0 - 4.0 * FILM_SPREAD) * value + FILM_SPREAD * ((n + s) + (ww + e))

        def substep(_, fields):
            height, along, across, heat = fields
            inverse = lax.rsqrt(height * height + FILM_FLOOR * FILM_FLOOR)
            hn, hs, hw, he = sides(height)
            un, us, uw, ue = sides(along)
            vn, vs, vw, ve = sides(across)
            tn, ts, tw, te = sides(heat)
            drag = (FRICTION * time_step) * inverse
            pull = (GRAVITY * half) * height
            return (
                spread(height, hn, hs, hw, he) + spray - half * ((ue - uw) + (vs - vn)),
                spread(along, un, us, uw, ue) + push_along - drag * along - pull * (he - hw),
                spread(across, vn, vs, vw, ve) + push_across - drag * across - pull * (hs - hn),
                spread(heat, tn, ts, tw, te) + heating * inverse,
            )

        fields = tuple(window(f) for f in range(4))
        fields = lax.fori_loop(0, SUBSTEPS, substep, fields)
        done = [pltpu.roll(value, block - HALO, 0)[0:strip, 0:cols] for value in fields]
        for f in range(4):
            outbox[i, f] = done[f]

        @pl.when(i < n_gas - 1)
        def _():
            strip_copy(i).start()

        return jnp.maximum(peak, tile_max(speed_measure(done[0], done[1], done[2])))

    last_peak = lax.fori_loop(
        0, n_gas, advance_strip, jnp.zeros((SUBLANES, LANES), jnp.float32)
    )
    peak_send[1, 0] = last_peak
    second_gas = gas_peaks(1)
    for copy in second_gas:
        copy.start()
    own = pltpu.make_async_copy(
        outbox.at[n_gas - 1],
        out_ref.at[:, :, pl.ds(pl.multiple_of(g * cols, LANES), cols)],
        own_sem,
    )
    own.start()
    second_wall = middle(1, last_peak, second_gas)
    cfl_ref[0, 0] = time_step * finish(1, second_wall)
    for copy in first_gas + first_wall + second_gas + second_wall:
        copy.wait_send()
    own.wait()
    for i in range(n_gas - 1):
        source = (g + n_gas - offset(i)) % n_gas
        arriving = pltpu.make_async_remote_copy(
            src_ref=outbox.at[i],
            dst_ref=out_ref.at[:, :, pl.ds(pl.multiple_of(source * cols, LANES), cols)],
            send_sem=strip_send.at[i],
            recv_sem=strip_recv.at[i],
            device_id=(w, (g + offset(i)) % n_gas),
            device_id_type=MESH,
        )
        arriving.wait_send()
        arriving.wait_recv()


def per_device(gas_state, wall_flags, film_state, deposit, owner_map):
    n_wall, n_gas = lax.axis_size("wall"), lax.axis_size("gas")
    rows, cols = film_state.shape[1], film_state.shape[2]
    strip = rows // n_gas
    tall, wide = rows + 2 * HALO, cols + LANES
    f32 = jnp.float32
    dma = pltpu.SemaphoreType.DMA
    film_out, cfl = pl.pallas_call(
        functools.partial(kernel, n_wall, n_gas),
        out_shape=(
            jax.ShapeDtypeStruct((4, strip, n_gas * cols), f32),
            jax.ShapeDtypeStruct((1, 1), f32),
        ),
        in_specs=[pl.BlockSpec(memory_space=pl.ANY)] * 5,
        out_specs=(
            pl.BlockSpec(memory_space=pl.ANY),
            pl.BlockSpec(memory_space=pltpu.SMEM),
        ),
        scratch_shapes=[
            pltpu.VMEM(gas_state.shape, f32),
            pltpu.VMEM(wall_flags.shape, jnp.int32),
            pltpu.VMEM(film_state.shape, f32),
            pltpu.VMEM(deposit.shape, f32),
            pltpu.SMEM(owner_map.shape, jnp.int32),
            pltpu.VMEM((FIELDS, tall, wide), f32),
            pltpu.VMEM((8, tall // SUBLANES, SUBLANES, wide), f32),
            pltpu.VMEM((n_gas, 4, strip, cols), f32),
            pltpu.VMEM((FIELDS, SUBLANES, cols), f32),
            pltpu.VMEM((FIELDS, SUBLANES, cols), f32),
            pltpu.VMEM((tall, LANES), f32),
            pltpu.VMEM((tall, LANES), f32),
            pltpu.VMEM((tall, LANES), f32),
            pltpu.VMEM((tall, LANES), f32),
            pltpu.VMEM((4, SUBLANES, LANES), f32),
            pltpu.VMEM((2, 2, SUBLANES, LANES), f32),
            pltpu.VMEM((2, n_gas - 1, SUBLANES, LANES), f32),
            pltpu.VMEM((2, n_wall - 1, SUBLANES, LANES), f32),
            dma((7,)),
            dma((8,)),
            dma((8,)),
            dma((2, n_gas - 1)),
            dma((2, n_gas - 1)),
            dma((2, n_wall - 1)),
            dma((2, n_wall - 1)),
            dma((n_gas - 1,)),
            dma((n_gas - 1,)),
            dma,
        ],
        compiler_params=pltpu.CompilerParams(
            collective_id=0, has_side_effects=True, vmem_limit_bytes=48 * 1024 * 1024
        ),
    )(gas_state, wall_flags, film_state, deposit, owner_map)
    return film_out, cfl.reshape(())


def solution(mesh):
    return jax.shard_map(
        per_device,
        mesh=mesh,
        in_specs=(
            P(None, None, "wall", "gas"),
            P("wall", "gas"),
            P(None, "wall", "gas"),
            P("wall", "gas"),
            P(),
        ),
        out_specs=(P(None, ("wall", "gas"), None), P()),
        check_vma=False,
    )
```

```python
import functools

import jax
import jax.numpy as jnp
from jax import lax
from jax.experimental import pallas as pl
from jax.experimental.pallas import tpu as pltpu
from jax.sharding import PartitionSpec as P

SUBSTEPS = 4
HALO = SUBSTEPS
LANES = 128
SUBLANES = 8

LAYER_WEIGHTS = (0.1, 0.2, 0.3, 0.4)
KAPPA = 0.41
HEIGHT_RATIO = 20.0
SPEED_FLOOR = 0.5
PRANDTL_TURB = 0.85
PRANDTL_JUMP = 3.0
LAMINAR_SHEAR = 0.3
LAMINAR_HEAT = 0.2
FILM_SPREAD = 0.24
FILM_FLOOR = 0.3
FRICTION = 0.5
GRAVITY = 1.0
COURANT = 6.0

FILM, GAS, DEPOSIT, ATTACHED, FIELDS = 0, 4, 7, 8, 9
MESH = pl.DeviceIdType.MESH


def reichardt(scaled_height):
    return jnp.log(1.0 + KAPPA * scaled_height) * (1.0 / KAPPA) + 7.8 * (
        1.0
        - jnp.exp(scaled_height * (-1.0 / 11.0))
        - scaled_height * (1.0 / 11.0) * jnp.exp(scaled_height * (-1.0 / 3.0))
    )


def speed_measure(height, along, across):
    squared = height * height + FILM_FLOOR * FILM_FLOOR
    inverse = lax.rsqrt(squared)
    thickness = squared * inverse
    return jnp.sqrt(along * along + across * across) * inverse + jnp.sqrt(GRAVITY * thickness)


def tile_max(value):
    tiles = [
        value[r : r + SUBLANES, c : c + LANES]
        for r in range(0, value.shape[0], SUBLANES)
        for c in range(0, value.shape[1], LANES)
    ]
    while len(tiles) > 1:
        tiles = [jnp.maximum(a, b) for a, b in zip(tiles[::2], tiles[1::2])] + (
            [tiles[-1]] if len(tiles) % 2 else []
        )
    return tiles[0]


def kernel(
    n_wall, n_gas,
    gas_hbm, flags_hbm, film_hbm, deposit_hbm, owner_hbm,
    out_ref, cfl_ref,
    gas, flags, film, deposit, owner, ext, held, outbox,
    from_north, from_south, pack_north, pack_south, east_side, west_side, pack_east, pack_west, corner,
    peak_send, peak_gas, peak_wall,
    load_sem, halo_send, halo_recv, peak_gas_send, peak_gas_recv, peak_wall_send, peak_wall_recv,
    strip_send, strip_recv, own_sem,
):
    rows, cols = film.shape[1], film.shape[2]
    wide = cols + LANES
    strip = rows // n_gas
    block = strip + 2 * HALO
    w, g = lax.axis_index("wall"), lax.axis_index("gas")
    north, south = (w + n_wall - 1) % n_wall, (w + 1) % n_wall
    west, east = (g + n_gas - 1) % n_gas, (g + 1) % n_gas

    loads = [
        pltpu.make_async_copy(film_hbm, film, load_sem.at[0]),
        pltpu.make_async_copy(flags_hbm, flags, load_sem.at[1]),
        pltpu.make_async_copy(deposit_hbm, deposit, load_sem.at[2]),
        pltpu.make_async_copy(owner_hbm, owner, load_sem.at[3]),
    ] + [
        pltpu.make_async_copy(gas_hbm.at[c], gas.at[c], load_sem.at[4 + c]) for c in range(3)
    ]
    for load in loads:
        load.start()

    barrier = pltpu.get_barrier_semaphore()
    peers = (
        [(w, (g + k) % n_gas) for k in range(1, n_gas)]
        + [((w + k) % n_wall, g) for k in range(1, n_wall)]
        + [(a, b) for a in (north, south) for b in (west, east)]
    )
    for peer in peers:
        pl.semaphore_signal(barrier, inc=1, device_id=peer, device_id_type=MESH)

    def gas_peaks(turn):
        return [
            pltpu.make_async_remote_copy(
                src_ref=peak_send.at[turn, 0],
                dst_ref=peak_gas.at[turn, k - 1],
                send_sem=peak_gas_send.at[turn, k - 1],
                recv_sem=peak_gas_recv.at[turn, k - 1],
                device_id=(w, (g + k) % n_gas),
                device_id_type=MESH,
            )
            for k in range(1, n_gas)
        ]

    def wall_peaks(turn):
        return [
            pltpu.make_async_remote_copy(
                src_ref=peak_send.at[turn, 1],
                dst_ref=peak_wall.at[turn, k - 1],
                send_sem=peak_wall_send.at[turn, k - 1],
                recv_sem=peak_wall_recv.at[turn, k - 1],
                device_id=((w + k) % n_wall, g),
                device_id_type=MESH,
            )
            for k in range(1, n_wall)
        ]

    def middle(turn, own_peak, copies):
        for copy in copies:
            copy.wait_recv()
        for k in range(n_gas - 1):
            own_peak = jnp.maximum(own_peak, peak_gas[turn, k])
        peak_send[turn, 1] = own_peak
        later = wall_peaks(turn)
        for copy in later:
            copy.start()
        return later

    def finish(turn, copies):
        for copy in copies:
            copy.wait_recv()
        whole = peak_send[turn, 1]
        for k in range(n_wall - 1):
            whole = jnp.maximum(whole, peak_wall[turn, k])
        return jnp.max(whole)

    loads[0].wait()
    peak_send[0, 0] = tile_max(speed_measure(film[0], film[1], film[2]))
    own_rows = slice(HALO, HALO + rows)
    for f in range(4):
        ext[FILM + f, own_rows, 0:cols] = film[f]
    loads[1].wait()
    lane_own = lax.broadcasted_iota(jnp.int32, (rows, LANES), 1)
    segments = cols // LANES
    counts = jnp.concatenate(
        [flags[...].astype(jnp.float32)] * -(-SUBLANES // segments), axis=0
    )
    counts = jnp.concatenate([counts] * (rows // counts.shape[0]), axis=0)
    counts = jnp.transpose(counts).astype(jnp.int32)
    for s in range(segments):
        ext[ATTACHED, own_rows, s * LANES : (s + 1) * LANES] = jnp.where(
            lane_own < counts[:, s : s + 1], 1.0, 0.0
        )
    loads[2].wait()
    ext[DEPOSIT, own_rows, 0:cols] = deposit[...]
    for c in range(3):
        loads[4 + c].wait()
        sampled = LAYER_WEIGHTS[0] * gas[c, 0]
        for layer in range(1, gas.shape[1]):
            sampled = sampled + LAYER_WEIGHTS[layer] * gas[c, layer]
        ext[GAS + c, own_rows, 0:cols] = sampled

    tall = rows + 2 * HALO
    lane = lax.broadcasted_iota(jnp.int32, (tall, LANES), 1)
    to_west = ext[0, :, 0:LANES]
    to_east = pltpu.roll(ext[0, :, cols - LANES : cols], HALO, 1)
    for f in range(1, FIELDS):
        here = lane >= HALO * f
        to_west = jnp.where(here, pltpu.roll(ext[f, :, 0:LANES], HALO * f, 1), to_west)
        to_east = jnp.where(
            here, pltpu.roll(ext[f, :, cols - LANES : cols], HALO * (f + 1), 1), to_east
        )
    pack_west[...] = to_west
    pack_east[...] = to_east
    upper = lax.broadcasted_iota(jnp.int32, (SUBLANES, cols), 0) < HALO
    for f in range(0, FIELDS, 2):
        low, high = ext[f, 0:SUBLANES, 0:cols], ext[f, tall - SUBLANES : tall, 0:cols]
        if f + 1 < FIELDS:
            low = jnp.where(upper, pltpu.roll(ext[f + 1, 0:SUBLANES, 0:cols], HALO, 0), low)
            high = jnp.where(
                upper, high, pltpu.roll(ext[f + 1, tall - SUBLANES : tall, 0:cols], HALO, 0)
            )
        pack_north[f // 2] = low
        pack_south[f // 2] = high

    pl.semaphore_wait(barrier, len(peers))
    first_gas = gas_peaks(0)
    for copy in first_gas:
        copy.start()

    top, bottom = pl.ds(0, SUBLANES), pl.ds(tall - SUBLANES, SUBLANES)

    def halo(index, src, dst, device):
        return pltpu.make_async_remote_copy(
            src_ref=src, dst_ref=dst, send_sem=halo_send.at[index], recv_sem=halo_recv.at[index],
            device_id=device, device_id_type=MESH,
        )

    halos = [
        halo(0, pack_north, from_south, (north, g)),
        halo(1, pack_south, from_north, (south, g)),
        halo(2, pack_west, east_side, (w, west)),
        halo(3, pack_east, west_side, (w, east)),
        halo(4, pack_west.at[top], corner.at[0], (north, west)),
        halo(5, pack_west.at[bottom], corner.at[1], (south, west)),
        halo(6, pack_east.at[top], corner.at[2], (north, east)),
        halo(7, pack_east.at[bottom], corner.at[3], (south, east)),
    ]
    for copy in halos:
        copy.start()

    first_wall = middle(0, peak_send[0, 0], first_gas)

    for copy in halos:
        copy.wait_recv()
    for f in range(FIELDS):
        above, below = from_north[f // 2], from_south[f // 2]
        if f % 2:
            above, below = pltpu.roll(above, HALO, 0), pltpu.roll(below, HALO, 0)
        ext[f, 0:HALO, 0:cols] = above[0:HALO]
        ext[f, tall - HALO : tall, 0:cols] = below[HALO : 2 * HALO]
    east_side[tall - HALO : tall] = corner[0, HALO : 2 * HALO]
    east_side[0:HALO] = corner[1, 0:HALO]
    west_side[tall - HALO : tall] = corner[2, HALO : 2 * HALO]
    west_side[0:HALO] = corner[3, 0:HALO]
    for f in range(FIELDS):
        ext[f, :, cols:wide] = jnp.where(
            lane < HALO,
            pltpu.roll(east_side[...], (LANES - HALO * f) % LANES, 1),
            pltpu.roll(west_side[...], LANES - HALO - HALO * f, 1),
        )

    tiles = tall // SUBLANES
    sub = lax.broadcasted_iota(jnp.int32, (SUBLANES, wide), 0)

    def tile_rows(i):
        start = i * SUBLANES
        return pl.ds(start if isinstance(i, int) else pl.multiple_of(start, SUBLANES), SUBLANES)

    def force_tile(i):
        now = tile_rows(i)
        above = tile_rows((i + tiles - 1) % tiles)
        below = tile_rows((i + 1) % tiles)

        def filtered(f):
            centre = ext[f, now, :]
            up = jnp.where(sub == 0, pltpu.roll(ext[f, above, :], 1, 0), pltpu.roll(centre, 1, 0))
            down = jnp.where(
                sub == SUBLANES - 1,
                pltpu.roll(ext[f, below, :], SUBLANES - 1, 0),
                pltpu.roll(centre, SUBLANES - 1, 0),
            )
            total = up + centre + down
            return (pltpu.roll(total, 1, 1) + total + pltpu.roll(total, wide - 1, 1)) * (1.0 / 9.0)

        along, across, gas_heat = filtered(GAS), filtered(GAS + 1), filtered(GAS + 2)
        attached = ext[ATTACHED, now, :] > 0.5
        wall_speed = jnp.sqrt(along * along + across * across + SPEED_FLOOR * SPEED_FLOOR)
        scaled_speed = reichardt(jnp.sqrt(HEIGHT_RATIO * wall_speed))
        contrast = gas_heat - ext[FILM + 3, now, :]
        factor = jnp.where(attached, wall_speed / (scaled_speed * scaled_speed), LAMINAR_SHEAR)
        for f in range(4):
            held[f, i] = ext[FILM + f, now, :]
        held[4, i] = factor * along
        held[5, i] = factor * across
        held[7, i] = ext[DEPOSIT, now, :]
        held[6, i] = contrast * jnp.where(
            attached, wall_speed / (PRANDTL_TURB * scaled_speed + PRANDTL_JUMP), LAMINAR_HEAT
        )

    def force_pair(i, carry):
        force_tile(2 * i)
        force_tile(2 * i + 1)
        return carry

    lax.fori_loop(0, tiles // 2, force_pair, 0)
    if tiles % 2:
        force_tile(tiles - 1)

    time_step = COURANT / finish(0, first_wall)
    half = 0.5 * time_step
    loads[3].wait()

    def offset(i):
        return n_gas // 2 + (i + 1) // 2 * (1 - 2 * (i % 2))

    def strip_copy(i):
        return pltpu.make_async_remote_copy(
            src_ref=outbox.at[i],
            dst_ref=out_ref.at[:, :, pl.ds(pl.multiple_of(g * cols, LANES), cols)],
            send_sem=strip_send.at[i],
            recv_sem=strip_recv.at[i],
            device_id=(w, (g + offset(i)) % n_gas),
            device_id_type=MESH,
        )

    def advance_strip(i, peak):
        target = (g + offset(i)) % n_gas
        which = jnp.int32(0)
        for j in range(n_gas):
            match = 1 - jnp.minimum(jnp.abs(owner[w, j] - target), 1)
            which = jnp.maximum(which, j * match)
        first = which * (strip // SUBLANES)

        def window(f):
            return jnp.concatenate([held[f, first + t] for t in range(block // SUBLANES)], axis=0)

        push_along = time_step * window(4)
        push_across = time_step * window(5)
        heating = time_step * window(6)
        spray = time_step * window(7)

        def sides(value):
            return (
                pltpu.roll(value, 1, 0),
                pltpu.roll(value, block - 1, 0),
                pltpu.roll(value, 1, 1),
                pltpu.roll(value, wide - 1, 1),
            )

        def spread(value, n, s, ww, e):
            return (1.0 - 4.0 * FILM_SPREAD) * value + FILM_SPREAD * ((n + s) + (ww + e))

        def substep(_, fields):
            height, along, across, heat = fields
            inverse = lax.rsqrt(height * height + FILM_FLOOR * FILM_FLOOR)
            hn, hs, hw, he = sides(height)
            un, us, uw, ue = sides(along)
            vn, vs, vw, ve = sides(across)
            tn, ts, tw, te = sides(heat)
            drag = (FRICTION * time_step) * inverse
            pull = (GRAVITY * half) * height
            return (
                spread(height, hn, hs, hw, he) + spray - half * ((ue - uw) + (vs - vn)),
                spread(along, un, us, uw, ue) + push_along - drag * along - pull * (he - hw),
                spread(across, vn, vs, vw, ve) + push_across - drag * across - pull * (hs - hn),
                spread(heat, tn, ts, tw, te) + heating * inverse,
            )

        fields = tuple(window(f) for f in range(4))
        fields = lax.fori_loop(0, SUBSTEPS, substep, fields)
        done = [pltpu.roll(value, block - HALO, 0)[0:strip, 0:cols] for value in fields]
        for f in range(4):
            outbox[i, f] = done[f]

        @pl.when(i < n_gas - 1)
        def _():
            strip_copy(i).start()

        return jnp.maximum(peak, tile_max(speed_measure(done[0], done[1], done[2])))

    last_peak = lax.fori_loop(
        0, n_gas, advance_strip, jnp.zeros((SUBLANES, LANES), jnp.float32)
    )
    peak_send[1, 0] = last_peak
    second_gas = gas_peaks(1)
    for copy in second_gas:
        copy.start()
    own = pltpu.make_async_copy(
        outbox.at[n_gas - 1],
        out_ref.at[:, :, pl.ds(pl.multiple_of(g * cols, LANES), cols)],
        own_sem,
    )
    own.start()
    second_wall = middle(1, last_peak, second_gas)
    cfl_ref[0, 0] = time_step * finish(1, second_wall)
    for copy in halos + first_gas + first_wall + second_gas + second_wall:
        copy.wait_send()
    own.wait()
    for i in range(n_gas - 1):
        source = (g + n_gas - offset(i)) % n_gas
        arriving = pltpu.make_async_remote_copy(
            src_ref=outbox.at[i],
            dst_ref=out_ref.at[:, :, pl.ds(pl.multiple_of(source * cols, LANES), cols)],
            send_sem=strip_send.at[i],
            recv_sem=strip_recv.at[i],
            device_id=(w, (g + offset(i)) % n_gas),
            device_id_type=MESH,
        )
        arriving.wait_send()
        arriving.wait_recv()


def per_device(gas_state, wall_flags, film_state, deposit, owner_map):
    n_wall, n_gas = lax.axis_size("wall"), lax.axis_size("gas")
    rows, cols = film_state.shape[1], film_state.shape[2]
    strip = rows // n_gas
    tall, wide = rows + 2 * HALO, cols + LANES
    f32 = jnp.float32
    dma = pltpu.SemaphoreType.DMA
    film_out, cfl = pl.pallas_call(
        functools.partial(kernel, n_wall, n_gas),
        out_shape=(
            jax.ShapeDtypeStruct((4, strip, n_gas * cols), f32),
            jax.ShapeDtypeStruct((1, 1), f32),
        ),
        in_specs=[pl.BlockSpec(memory_space=pltpu.HBM)] * 5,
        out_specs=(
            pl.BlockSpec(memory_space=pltpu.HBM),
            pl.BlockSpec(memory_space=pltpu.SMEM),
        ),
        scratch_shapes=[
            pltpu.VMEM(gas_state.shape, f32),
            pltpu.VMEM(wall_flags.shape[::-1], jnp.int32),
            pltpu.VMEM(film_state.shape, f32),
            pltpu.VMEM(deposit.shape, f32),
            pltpu.SMEM(owner_map.shape, jnp.int32),
            pltpu.VMEM((FIELDS, tall, wide), f32),
            pltpu.VMEM((8, tall // SUBLANES, SUBLANES, wide), f32),
            pltpu.VMEM((n_gas, 4, strip, cols), f32),
            pltpu.VMEM((-(-FIELDS // 2), SUBLANES, cols), f32),
            pltpu.VMEM((-(-FIELDS // 2), SUBLANES, cols), f32),
            pltpu.VMEM((-(-FIELDS // 2), SUBLANES, cols), f32),
            pltpu.VMEM((-(-FIELDS // 2), SUBLANES, cols), f32),
            pltpu.VMEM((tall, LANES), f32),
            pltpu.VMEM((tall, LANES), f32),
            pltpu.VMEM((tall, LANES), f32),
            pltpu.VMEM((tall, LANES), f32),
            pltpu.VMEM((4, SUBLANES, LANES), f32),
            pltpu.VMEM((2, 2, SUBLANES, LANES), f32),
            pltpu.VMEM((2, n_gas - 1, SUBLANES, LANES), f32),
            pltpu.VMEM((2, n_wall - 1, SUBLANES, LANES), f32),
            dma((7,)),
            dma((8,)),
            dma((8,)),
            dma((2, n_gas - 1)),
            dma((2, n_gas - 1)),
            dma((2, n_wall - 1)),
            dma((2, n_wall - 1)),
            dma((n_gas - 1,)),
            dma((n_gas - 1,)),
            dma,
        ],
        compiler_params=pltpu.CompilerParams(
            collective_id=0, has_side_effects=True, vmem_limit_bytes=60 * 1024 * 1024
        ),
    )(gas_state, wall_flags.T, film_state, deposit, owner_map)
    return film_out, cfl.reshape(())


def solution(mesh):
    return jax.shard_map(
        per_device,
        mesh=mesh,
        in_specs=(
            P(None, None, "wall", "gas"),
            P("wall", "gas"),
            P(None, "wall", "gas"),
            P("wall", "gas"),
            P(),
        ),
        out_specs=(P(None, ("wall", "gas"), None), P()),
        check_vma=False,
    )
```

```python
import functools

import jax
import jax.numpy as jnp
from jax import lax
from jax.experimental import pallas as pl
from jax.experimental.pallas import tpu as pltpu
from jax.sharding import PartitionSpec as P

SUBSTEPS = 4
HALO = SUBSTEPS
LANES = 128
SUBLANES = 8

LAYER_WEIGHTS = (0.1, 0.2, 0.3, 0.4)
KAPPA = 0.41
HEIGHT_RATIO = 20.0
SPEED_FLOOR = 0.5
PRANDTL_TURB = 0.85
PRANDTL_JUMP = 3.0
LAMINAR_SHEAR = 0.3
LAMINAR_HEAT = 0.2
FILM_SPREAD = 0.24
FILM_FLOOR = 0.3
FRICTION = 0.5
GRAVITY = 1.0
COURANT = 6.0

FILM, GAS, DEPOSIT, ATTACHED, FIELDS = 0, 4, 7, 8, 9
MESH = pl.DeviceIdType.MESH


def reichardt(scaled_height):
    return jnp.log(1.0 + KAPPA * scaled_height) * (1.0 / KAPPA) + 7.8 * (
        1.0
        - jnp.exp(scaled_height * (-1.0 / 11.0))
        - scaled_height * (1.0 / 11.0) * jnp.exp(scaled_height * (-1.0 / 3.0))
    )


def speed_measure(height, along, across):
    squared = height * height + FILM_FLOOR * FILM_FLOOR
    inverse = lax.rsqrt(squared)
    thickness = squared * inverse
    return jnp.sqrt(along * along + across * across) * inverse + jnp.sqrt(GRAVITY * thickness)


def tile_max(value):
    tiles = [
        value[r : r + SUBLANES, c : c + LANES]
        for r in range(0, value.shape[0], SUBLANES)
        for c in range(0, value.shape[1], LANES)
    ]
    while len(tiles) > 1:
        tiles = [jnp.maximum(a, b) for a, b in zip(tiles[::2], tiles[1::2])] + (
            [tiles[-1]] if len(tiles) % 2 else []
        )
    return tiles[0]


def kernel(
    n_wall, n_gas,
    gas_hbm, flags_hbm, film_hbm, deposit_hbm, owner_hbm,
    out_ref, cfl_ref,
    gas, flags, film, deposit, owner, ext, held, outbox,
    from_north, from_south, pack_north, pack_south, east_side, west_side, pack_east, pack_west, corner,
    peak_send, peak_gas, peak_wall,
    load_sem, halo_send, halo_recv, peak_gas_send, peak_gas_recv, peak_wall_send, peak_wall_recv,
    strip_send, strip_recv, own_sem,
):
    rows, cols = film.shape[1], film.shape[2]
    wide = cols + LANES
    strip = rows // n_gas
    block = strip + 2 * HALO
    w, g = lax.axis_index("wall"), lax.axis_index("gas")
    north, south = (w + n_wall - 1) % n_wall, (w + 1) % n_wall
    west, east = (g + n_gas - 1) % n_gas, (g + 1) % n_gas

    loads = [
        pltpu.make_async_copy(film_hbm, film, load_sem.at[0]),
        pltpu.make_async_copy(flags_hbm, flags, load_sem.at[1]),
        pltpu.make_async_copy(deposit_hbm, deposit, load_sem.at[2]),
        pltpu.make_async_copy(owner_hbm, owner, load_sem.at[3]),
    ] + [
        pltpu.make_async_copy(gas_hbm.at[c], gas.at[c], load_sem.at[4 + c]) for c in range(3)
    ]
    for load in loads:
        load.start()

    barrier = pltpu.get_barrier_semaphore()
    peers = (
        [(w, (g + k) % n_gas) for k in range(1, n_gas)]
        + [((w + k) % n_wall, g) for k in range(1, n_wall)]
        + [(a, b) for a in (north, south) for b in (west, east)]
    )
    for peer in peers:
        pl.semaphore_signal(barrier, inc=1, device_id=peer, device_id_type=MESH)

    def gas_peaks(turn):
        return [
            pltpu.make_async_remote_copy(
                src_ref=peak_send.at[turn, turn],
                dst_ref=peak_gas.at[turn, k - 1],
                send_sem=peak_gas_send.at[turn, k - 1],
                recv_sem=peak_gas_recv.at[turn, k - 1],
                device_id=(w, (g + k) % n_gas),
                device_id_type=MESH,
            )
            for k in range(1, n_gas)
        ]

    def wall_peaks(turn):
        return [
            pltpu.make_async_remote_copy(
                src_ref=peak_send.at[turn, 1 - turn],
                dst_ref=peak_wall.at[turn, k - 1],
                send_sem=peak_wall_send.at[turn, k - 1],
                recv_sem=peak_wall_recv.at[turn, k - 1],
                device_id=((w + k) % n_wall, g),
                device_id_type=MESH,
            )
            for k in range(1, n_wall)
        ]

    def gather_peaks(turn, own_peak, copies, landed):
        for copy in copies:
            copy.wait_recv()
        for k in range(len(copies)):
            own_peak = jnp.maximum(own_peak, landed[turn, k])
        return own_peak

    loads[0].wait()
    peak_send[0, 0] = tile_max(speed_measure(film[0], film[1], film[2]))
    own_rows = slice(HALO, HALO + rows)
    for f in range(4):
        ext[FILM + f, own_rows, 0:cols] = film[f]
    loads[1].wait()
    lane_own = lax.broadcasted_iota(jnp.int32, (rows, LANES), 1)
    segments = cols // LANES
    counts = jnp.concatenate(
        [flags[...].astype(jnp.float32)] * -(-SUBLANES // segments), axis=0
    )
    counts = jnp.concatenate([counts] * (rows // counts.shape[0]), axis=0)
    counts = jnp.transpose(counts).astype(jnp.int32)
    for s in range(segments):
        ext[ATTACHED, own_rows, s * LANES : (s + 1) * LANES] = jnp.where(
            lane_own < counts[:, s : s + 1], 1.0, 0.0
        )
    loads[2].wait()
    ext[DEPOSIT, own_rows, 0:cols] = deposit[...]
    for c in range(3):
        loads[4 + c].wait()
        sampled = LAYER_WEIGHTS[0] * gas[c, 0]
        for layer in range(1, gas.shape[1]):
            sampled = sampled + LAYER_WEIGHTS[layer] * gas[c, layer]
        ext[GAS + c, own_rows, 0:cols] = sampled

    tall = rows + 2 * HALO
    lane = lax.broadcasted_iota(jnp.int32, (tall, LANES), 1)
    to_west = ext[0, :, 0:LANES]
    to_east = pltpu.roll(ext[0, :, cols - LANES : cols], HALO, 1)
    for f in range(1, FIELDS):
        here = lane >= HALO * f
        to_west = jnp.where(here, pltpu.roll(ext[f, :, 0:LANES], HALO * f, 1), to_west)
        to_east = jnp.where(
            here, pltpu.roll(ext[f, :, cols - LANES : cols], HALO * (f + 1), 1), to_east
        )
    pack_west[...] = to_west
    pack_east[...] = to_east
    upper = lax.broadcasted_iota(jnp.int32, (SUBLANES, cols), 0) < HALO
    for f in range(0, FIELDS, 2):
        low, high = ext[f, 0:SUBLANES, 0:cols], ext[f, tall - SUBLANES : tall, 0:cols]
        if f + 1 < FIELDS:
            low = jnp.where(upper, pltpu.roll(ext[f + 1, 0:SUBLANES, 0:cols], HALO, 0), low)
            high = jnp.where(
                upper, high, pltpu.roll(ext[f + 1, tall - SUBLANES : tall, 0:cols], HALO, 0)
            )
        pack_north[f // 2] = low
        pack_south[f // 2] = high

    pl.semaphore_wait(barrier, len(peers))
    first_gas = gas_peaks(0)
    for copy in first_gas:
        copy.start()

    top, bottom = pl.ds(0, SUBLANES), pl.ds(tall - SUBLANES, SUBLANES)

    def halo(index, src, dst, device):
        return pltpu.make_async_remote_copy(
            src_ref=src, dst_ref=dst, send_sem=halo_send.at[index], recv_sem=halo_recv.at[index],
            device_id=device, device_id_type=MESH,
        )

    halos = [
        halo(0, pack_north, from_south, (north, g)),
        halo(1, pack_south, from_north, (south, g)),
        halo(2, pack_west, east_side, (w, west)),
        halo(3, pack_east, west_side, (w, east)),
        halo(4, pack_west.at[top], corner.at[0], (north, west)),
        halo(5, pack_west.at[bottom], corner.at[1], (south, west)),
        halo(6, pack_east.at[top], corner.at[2], (north, east)),
        halo(7, pack_east.at[bottom], corner.at[3], (south, east)),
    ]
    for copy in halos:
        copy.start()

    peak_send[0, 1] = gather_peaks(0, peak_send[0, 0], first_gas, peak_gas)
    first_wall = wall_peaks(0)
    for copy in first_wall:
        copy.start()

    for copy in halos:
        copy.wait_recv()
    for f in range(FIELDS):
        above, below = from_north[f // 2], from_south[f // 2]
        if f % 2:
            above, below = pltpu.roll(above, HALO, 0), pltpu.roll(below, HALO, 0)
        ext[f, 0:HALO, 0:cols] = above[0:HALO]
        ext[f, tall - HALO : tall, 0:cols] = below[HALO : 2 * HALO]
    east_side[tall - HALO : tall] = corner[0, HALO : 2 * HALO]
    east_side[0:HALO] = corner[1, 0:HALO]
    west_side[tall - HALO : tall] = corner[2, HALO : 2 * HALO]
    west_side[0:HALO] = corner[3, 0:HALO]
    for f in range(FIELDS):
        ext[f, :, cols:wide] = jnp.where(
            lane < HALO,
            pltpu.roll(east_side[...], (LANES - HALO * f) % LANES, 1),
            pltpu.roll(west_side[...], LANES - HALO - HALO * f, 1),
        )

    tiles = tall // SUBLANES
    sub = lax.broadcasted_iota(jnp.int32, (SUBLANES, wide), 0)

    def tile_rows(i):
        start = i * SUBLANES
        return pl.ds(start if isinstance(i, int) else pl.multiple_of(start, SUBLANES), SUBLANES)

    def force_tile(i):
        now = tile_rows(i)
        above = tile_rows((i + tiles - 1) % tiles)
        below = tile_rows((i + 1) % tiles)

        def filtered(f):
            centre = ext[f, now, :]
            up = jnp.where(sub == 0, pltpu.roll(ext[f, above, :], 1, 0), pltpu.roll(centre, 1, 0))
            down = jnp.where(
                sub == SUBLANES - 1,
                pltpu.roll(ext[f, below, :], SUBLANES - 1, 0),
                pltpu.roll(centre, SUBLANES - 1, 0),
            )
            total = up + centre + down
            return (pltpu.roll(total, 1, 1) + total + pltpu.roll(total, wide - 1, 1)) * (1.0 / 9.0)

        along, across, gas_heat = filtered(GAS), filtered(GAS + 1), filtered(GAS + 2)
        attached = ext[ATTACHED, now, :] > 0.5
        wall_speed = jnp.sqrt(along * along + across * across + SPEED_FLOOR * SPEED_FLOOR)
        scaled_speed = reichardt(jnp.sqrt(HEIGHT_RATIO * wall_speed))
        contrast = gas_heat - ext[FILM + 3, now, :]
        factor = jnp.where(attached, wall_speed / (scaled_speed * scaled_speed), LAMINAR_SHEAR)
        for f in range(4):
            held[f, i] = ext[FILM + f, now, :]
        held[4, i] = factor * along
        held[5, i] = factor * across
        held[7, i] = ext[DEPOSIT, now, :]
        held[6, i] = contrast * jnp.where(
            attached, wall_speed / (PRANDTL_TURB * scaled_speed + PRANDTL_JUMP), LAMINAR_HEAT
        )

    def force_pair(i, carry):
        force_tile(2 * i)
        force_tile(2 * i + 1)
        return carry

    lax.fori_loop(0, tiles // 2, force_pair, 0)
    if tiles % 2:
        force_tile(tiles - 1)

    time_step = COURANT / jnp.max(
        gather_peaks(0, peak_send[0, 1], first_wall, peak_wall)
    )
    half = 0.5 * time_step
    loads[3].wait()

    def offset(i):
        return n_gas // 2 + (i + 1) // 2 * (1 - 2 * (i % 2))

    def strip_copy(i):
        return pltpu.make_async_remote_copy(
            src_ref=outbox.at[i],
            dst_ref=out_ref.at[:, :, pl.ds(pl.multiple_of(g * cols, LANES), cols)],
            send_sem=strip_send.at[i],
            recv_sem=strip_recv.at[i],
            device_id=(w, (g + offset(i)) % n_gas),
            device_id_type=MESH,
        )

    def advance_strip(i, peak):
        target = (g + offset(i)) % n_gas
        which = jnp.int32(0)
        for j in range(n_gas):
            match = 1 - jnp.minimum(jnp.abs(owner[w, j] - target), 1)
            which = jnp.maximum(which, j * match)
        first = which * (strip // SUBLANES)

        def window(f):
            return jnp.concatenate([held[f, first + t] for t in range(block // SUBLANES)], axis=0)

        push_along = time_step * window(4)
        push_across = time_step * window(5)
        heating = time_step * window(6)
        spray = time_step * window(7)

        def sides(value):
            return (
                pltpu.roll(value, 1, 0),
                pltpu.roll(value, block - 1, 0),
                pltpu.roll(value, 1, 1),
                pltpu.roll(value, wide - 1, 1),
            )

        def spread(value, n, s, ww, e):
            return (1.0 - 4.0 * FILM_SPREAD) * value + FILM_SPREAD * ((n + s) + (ww + e))

        def substep(_, fields):
            height, along, across, heat = fields
            inverse = lax.rsqrt(height * height + FILM_FLOOR * FILM_FLOOR)
            hn, hs, hw, he = sides(height)
            un, us, uw, ue = sides(along)
            vn, vs, vw, ve = sides(across)
            tn, ts, tw, te = sides(heat)
            drag = (FRICTION * time_step) * inverse
            pull = (GRAVITY * half) * height
            return (
                spread(height, hn, hs, hw, he) + spray - half * ((ue - uw) + (vs - vn)),
                spread(along, un, us, uw, ue) + push_along - drag * along - pull * (he - hw),
                spread(across, vn, vs, vw, ve) + push_across - drag * across - pull * (hs - hn),
                spread(heat, tn, ts, tw, te) + heating * inverse,
            )

        fields = tuple(window(f) for f in range(4))
        fields = lax.fori_loop(0, SUBSTEPS, substep, fields)
        done = [pltpu.roll(value, block - HALO, 0)[0:strip, 0:cols] for value in fields]
        for f in range(4):
            outbox[i, f] = done[f]

        @pl.when(i < n_gas - 1)
        def _():
            strip_copy(i).start()

        return jnp.maximum(peak, tile_max(speed_measure(done[0], done[1], done[2])))

    last_peak = lax.fori_loop(
        0, n_gas, advance_strip, jnp.zeros((SUBLANES, LANES), jnp.float32)
    )
    peak_send[1, 0] = last_peak
    second_wall = wall_peaks(1)
    for copy in second_wall:
        copy.start()
    own = pltpu.make_async_copy(
        outbox.at[n_gas - 1],
        out_ref.at[:, :, pl.ds(pl.multiple_of(g * cols, LANES), cols)],
        own_sem,
    )
    own.start()
    peak_send[1, 1] = gather_peaks(1, last_peak, second_wall, peak_wall)
    second_gas = gas_peaks(1)
    for copy in second_gas:
        copy.start()
    cfl_ref[0, 0] = time_step * jnp.max(
        gather_peaks(1, peak_send[1, 1], second_gas, peak_gas)
    )
    for copy in halos + first_gas + first_wall + second_gas + second_wall:
        copy.wait_send()
    own.wait()
    for i in range(n_gas - 1):
        source = (g + n_gas - offset(i)) % n_gas
        arriving = pltpu.make_async_remote_copy(
            src_ref=outbox.at[i],
            dst_ref=out_ref.at[:, :, pl.ds(pl.multiple_of(source * cols, LANES), cols)],
            send_sem=strip_send.at[i],
            recv_sem=strip_recv.at[i],
            device_id=(w, (g + offset(i)) % n_gas),
            device_id_type=MESH,
        )
        arriving.wait_send()
        arriving.wait_recv()


def per_device(gas_state, wall_flags, film_state, deposit, owner_map):
    n_wall, n_gas = lax.axis_size("wall"), lax.axis_size("gas")
    rows, cols = film_state.shape[1], film_state.shape[2]
    strip = rows // n_gas
    tall, wide = rows + 2 * HALO, cols + LANES
    f32 = jnp.float32
    dma = pltpu.SemaphoreType.DMA
    film_out, cfl = pl.pallas_call(
        functools.partial(kernel, n_wall, n_gas),
        out_shape=(
            jax.ShapeDtypeStruct((4, strip, n_gas * cols), f32),
            jax.ShapeDtypeStruct((1, 1), f32),
        ),
        in_specs=[pl.BlockSpec(memory_space=pltpu.HBM)] * 5,
        out_specs=(
            pl.BlockSpec(memory_space=pltpu.HBM),
            pl.BlockSpec(memory_space=pltpu.SMEM),
        ),
        scratch_shapes=[
            pltpu.VMEM(gas_state.shape, f32),
            pltpu.VMEM(wall_flags.shape[::-1], jnp.int32),
            pltpu.VMEM(film_state.shape, f32),
            pltpu.VMEM(deposit.shape, f32),
            pltpu.SMEM(owner_map.shape, jnp.int32),
            pltpu.VMEM((FIELDS, tall, wide), f32),
            pltpu.VMEM((8, tall // SUBLANES, SUBLANES, wide), f32),
            pltpu.VMEM((n_gas, 4, strip, cols), f32),
            pltpu.VMEM((-(-FIELDS // 2), SUBLANES, cols), f32),
            pltpu.VMEM((-(-FIELDS // 2), SUBLANES, cols), f32),
            pltpu.VMEM((-(-FIELDS // 2), SUBLANES, cols), f32),
            pltpu.VMEM((-(-FIELDS // 2), SUBLANES, cols), f32),
            pltpu.VMEM((tall, LANES), f32),
            pltpu.VMEM((tall, LANES), f32),
            pltpu.VMEM((tall, LANES), f32),
            pltpu.VMEM((tall, LANES), f32),
            pltpu.VMEM((4, SUBLANES, LANES), f32),
            pltpu.VMEM((2, 2, SUBLANES, LANES), f32),
            pltpu.VMEM((2, n_gas - 1, SUBLANES, LANES), f32),
            pltpu.VMEM((2, n_wall - 1, SUBLANES, LANES), f32),
            dma((7,)),
            dma((8,)),
            dma((8,)),
            dma((2, n_gas - 1)),
            dma((2, n_gas - 1)),
            dma((2, n_wall - 1)),
            dma((2, n_wall - 1)),
            dma((n_gas - 1,)),
            dma((n_gas - 1,)),
            dma,
        ],
        compiler_params=pltpu.CompilerParams(
            collective_id=0, has_side_effects=True, vmem_limit_bytes=60 * 1024 * 1024
        ),
    )(gas_state, wall_flags.T, film_state, deposit, owner_map)
    return film_out, cfl.reshape(())


def solution(mesh):
    return jax.shard_map(
        per_device,
        mesh=mesh,
        in_specs=(
            P(None, None, "wall", "gas"),
            P("wall", "gas"),
            P(None, "wall", "gas"),
            P("wall", "gas"),
            P(),
        ),
        out_specs=(P(None, ("wall", "gas"), None), P()),
        check_vma=False,
    )
```
